128 devices in a mesh: section: 4 (over z_hi, core), win: 32 (over z_lo, y, x).
Axes of the slice: x: 4, y: 4, z: 4 (z_hi: 2, z_lo: 2; z = z_hi * 2 + z_lo), core: 2. Of those that a mesh axis runs over, the one named last changes fastest.
Arguments:
- latent: bfloat16 [24, 256, 256], P(None, 'win'), may hold values from -6 to 6
- anchors: int32 [64, 2], P('win'), may hold values from 0 to 248, as said below
- in_proj: bfloat16 [256, 1280], replicated, may hold values from -0.375 to 0.375
- pos_embed: bfloat16 [256, 1280], replicated, may hold values from -6 to 6
- section_w1: bfloat16 [4, 1280, 2560], P('section'), may hold values from -0.15625 to 0.15625
- section_w2: bfloat16 [4, 2560, 1280], P('section'), may hold values from -0.125 to 0.125
- section_gain: float32 [4, 1280], P('section'), may hold values from 0.5 to 1.5
- skip_w: bfloat16 [2560, 1280], replicated, may hold values from -0.125 to 0.125
- out_proj: bfloat16 [1280, 256], replicated, may hold values from -0.15625 to 0.15625
Outputs:
- noise_avg: bfloat16 [24, 256, 256], P('section', 'win')
The draws below stay inside these ranges and needn't reach their ends.
Inputs may be any that keep to these rules, and one draw needn't show every extreme that they name: Column 0 holds the row anchor, column 1 the column anchor; the windows are listed in an order drawn at random. Every column anchor that is a multiple of 8 below 256 appears in exactly 2 windows. Let g be a column anchor divided by 8. For even g, the row anchors of those windows are 0 and 8. For odd g, each row anchor lies anywhere from 0 to 8. Every token is covered by at least one window.
All inputs are finite; a program needn't handle non-finite values.
Results may differ from the reference program's by a relative error of at most 0.014.
Values may be sent and summed in bfloat16 or wider, within the bound.
No kernel may reach another device: no remote copies, remote signals or barrier semaphores. Data moves between devices by JAX's collectives and lax.ppermute only.
A program may use at most 128 MiB of HBM per device.

```python
import jax
import jax.numpy as jnp
from jax import lax

D = 1280
HID = 2560
FEAT = 256
TILE = 16
STRIDE = 8
SECTIONS = 4
PW = 256
PH = 24
WINDOWS = 64


def draw_anchors(key, part):
    key = jax.random.fold_in(key, 11)
    order = jax.random.permutation(jax.random.fold_in(key, 1), WINDOWS)
    across = PW // STRIDE
    slot = order // across
    grid = order % across
    moved_row = jax.random.randint(jax.random.fold_in(key, 2), (WINDOWS,), 0, PH - TILE + 1)
    row_anchor = jnp.where(grid % 2 == 0, slot * STRIDE, moved_row)
    col_anchor = grid * STRIDE
    return jnp.stack([row_anchor, col_anchor], axis=1).astype(jnp.int32)


def block_levels(own_key, extent, split, low, top_value):
    level = 1.0
    for position, parts in split:
        draws = jax.random.uniform(jax.random.fold_in(jax.random.fold_in(own_key, 6), position), (parts,), jnp.float32, low / len(split), top_value / len(split))
        level = level * jnp.repeat(jnp.exp(draws), extent[position] // parts).reshape((-1,) + (1,) * (len(extent) - 1 - position))
    return level


def normal_values(rng, dims, deviation, limit, pieces=(), kind=jnp.bfloat16):
    values = jax.random.normal(rng, dims, jnp.float32) * deviation
    if len(pieces) > 0:
        values = block_levels(rng, dims, pieces, -0.22, 0.18) * values
    return jnp.clip(values, min=-limit, max=limit).astype(kind)


def setup_inputs(seed: int = 0) -> dict:
    key_of = jax.random.split(jax.random.key(seed), 10)
    latent = normal_values(key_of[0], (PH, PW, FEAT), 1.0, 6.0, ((1, 32),))
    anchors = draw_anchors(jax.random.fold_in(key_of[9], 71), 0)
    in_proj = normal_values(key_of[2], (FEAT, D), FEAT ** -0.5, 0.375)
    pos_embed = normal_values(key_of[3], (TILE * TILE, D), 1.0, 6.0)
    section_w1 = normal_values(key_of[4], (SECTIONS, D, HID), D ** -0.5, 0.15625, ((0, 4),))
    section_w2 = normal_values(key_of[5], (SECTIONS, HID, D), HID ** -0.5, 0.125, ((0, 4),))
    section_gain = jnp.clip(1.0 + 0.1 * jax.random.normal(key_of[6], (SECTIONS, D), jnp.float32), 0.5, 1.5)
    skip_w = normal_values(key_of[7], (2 * D, D), (2 * D) ** -0.5, 0.125)
    out_proj = normal_values(key_of[8], (D, FEAT), D ** -0.5, 0.15625)
    return {"latent": latent, "anchors": anchors, "in_proj": in_proj, "pos_embed": pos_embed, "section_w1": section_w1, "section_w2": section_w2, "section_gain": section_gain, "skip_w": skip_w, "out_proj": out_proj}


def rms_block(values, gain, w_first, w_second):
    factor = lax.rsqrt(lax.optimization_barrier(jnp.mean(values * values, axis=-1, keepdims=True)) + 1e-06)
    normed = (values * factor * gain).astype(jnp.bfloat16)
    hidden = jax.nn.gelu(jnp.dot(normed, w_first, preferred_element_type=jnp.float32), approximate=True).astype(jnp.bfloat16)
    return values + jnp.dot(hidden, w_second, preferred_element_type=jnp.float32)

def reference(latent, anchors, in_proj, pos_embed, section_w1, section_w2, section_gain, skip_w, out_proj):
    offsets = jnp.arange(TILE, dtype=jnp.int32)
    position_term = pos_embed.astype(jnp.float32)

    def one_window(anchor):
        row_index = anchor[0] + offsets
        col_index = (anchor[1] + offsets) % PW
        tiles = latent[row_index[:, None], col_index[None, :]].reshape(TILE * TILE, FEAT)
        embedded = jnp.dot(tiles, in_proj, preferred_element_type=jnp.float32) + position_term
        first = rms_block(embedded, section_gain[0], section_w1[0], section_w2[0]).astype(jnp.bfloat16)
        second = rms_block(first.astype(jnp.float32), section_gain[1], section_w1[1], section_w2[1]).astype(jnp.bfloat16)
        third = rms_block(second.astype(jnp.float32), section_gain[2], section_w1[2], section_w2[2]).astype(jnp.bfloat16)
        merged = jnp.dot(jnp.concatenate([third, first], axis=1), skip_w, preferred_element_type=jnp.float32)
        deep = rms_block(merged, section_gain[3], section_w1[3], section_w2[3]).astype(jnp.bfloat16)
        return jnp.dot(deep, out_proj, preferred_element_type=jnp.float32).astype(jnp.bfloat16)
    noises = lax.map(one_window, anchors)
    row_index = anchors[:, 0:1] + offsets[None, :]
    col_index = (anchors[:, 1:2] + offsets[None, :]) % PW
    placed = noises.reshape(WINDOWS, TILE, TILE, FEAT).astype(jnp.float32)
    totals = jnp.zeros((PH, PW, FEAT), jnp.float32).at[row_index[:, :, None], col_index[:, None, :]].add(placed)
    covered = jnp.zeros((PH, PW), jnp.float32).at[row_index[:, :, None], col_index[:, None, :]].add(1.0)
    return (totals / covered[..., None]).astype(jnp.bfloat16)
```

```python
import functools

import jax
import jax.numpy as jnp
from jax import lax
from jax.experimental import pallas as pl
from jax.experimental.pallas import tpu as pltpu
from jax.sharding import PartitionSpec as P

TILE = 16
STRIDE = 8
HALF = TILE // 2
MIB = 1 << 20
F32 = jnp.float32
BF16 = jnp.bfloat16


def gelu(v):
    return jax.nn.gelu(v, approximate=True)


def normalise(v, gain):
    factor = lax.rsqrt(jnp.mean(v * v, axis=-1, keepdims=True) + 1e-06)
    return (v * factor * gain).astype(BF16)


def embed_rows(lat, inp, pos, anchor, half):
    rows = lat[pl.ds(anchor, TILE)].astype(F32)
    tiles = rows.reshape(TILE * HALF, rows.shape[-1]).astype(BF16)
    place = pos[:, half].astype(F32).reshape(TILE * HALF, pos.shape[-1])
    return jnp.dot(tiles, inp[...], preferred_element_type=F32) + place


def load_kernel(
    chunks, meta, lat_h, inp_h, pos_h, gain_h, w1_h, w2_h, skip_h, outp_h,
    y, lat, inp, pos, gain_ref, w1, w2, skip, outp, norm, acc, sems,
):
    section, half = meta[0], meta[1]
    hidden = w1.shape[1]
    size = hidden // chunks
    small = [(lat_h, lat), (inp_h, inp), (pos_h, pos), (gain_h, gain_ref), (outp_h, outp)]
    copies = [pltpu.make_async_copy(a, b, sems.at[k]) for k, (a, b) in enumerate(small)]
    base = len(small)
    for c in range(chunks):
        cut = pl.ds(c * size, size)
        copies.append(pltpu.make_async_copy(w1_h.at[0, :, cut], w1.at[:, cut], sems.at[base + 2 * c]))
        copies.append(pltpu.make_async_copy(w2_h.at[0, cut, :], w2.at[cut, :], sems.at[base + 2 * c + 1]))
    for copy in copies:
        copy.start()
    last = base + 2 * chunks

    @pl.when(section == 3)
    def _():
        pltpu.make_async_copy(skip_h, skip, sems.at[last]).start()

    for k in range(base):
        copies[k].wait()

    @pl.when(section == 0)
    def _():
        v = embed_rows(lat, inp, pos, 0, half)
        acc[...] = v
        norm[...] = normalise(v, gain_ref[...])

    for c in range(chunks):
        cut = pl.ds(c * size, size)
        copies[base + 2 * c].wait()
        copies[base + 2 * c + 1].wait()

        @pl.when(section == 0)
        def _():
            h = gelu(jnp.dot(norm[...], w1[:, cut], preferred_element_type=F32)).astype(BF16)
            acc[...] += jnp.dot(h, w2[cut, :], preferred_element_type=F32)

    @pl.when(section == 0)
    def _():
        y[...] = acc[...].astype(BF16)

    @pl.when(section == 3)
    def _():
        pltpu.make_async_copy(skip_h, skip, sems.at[last]).wait()


def join_kernel(left, right, out):
    a, b = left[...], right[...]
    first = lax.broadcasted_iota(jnp.int32, a.shape, 0) == 0
    out[...] = jnp.where(first, a + b, jnp.maximum(a, b))


def tick_kernel(roles, names, outs, *refs):
    at = dict(zip(names, refs))
    meta = at["meta"]
    section, parity = meta[0], meta[1]
    norm, acc = at["norm"], at["acc"]
    w1, w2 = at["w1"], at["w2"]
    dim, hidden = w1.shape

    def anchor_of(part):
        if part < 2:
            return part * STRIDE
        top = at["table"][1, meta[2]]
        return top if part == 2 else at["table"][0, meta[2]] - top

    if roles[0] is not None:

        @pl.when(section == 0)
        def _():
            part = roles[0]
            half = parity if part < 2 else 1 - parity
            acc[...] = embed_rows(at["lat"], at["inp"], at["pos"], anchor_of(part), half)

    if roles[1] is not None:

        @pl.when(section == 1)
        def _():
            acc[...] = at["near"][...].astype(F32)

    if roles[2] is not None:

        @pl.when(section == 2)
        def _():
            acc[...] = at["far"][...].astype(F32)

    if roles[3] is not None:

        @pl.when(section == 3)
        def _():
            acc[...] = jnp.dot(
                at["near"][...], at["skip"][:dim, :], preferred_element_type=F32
            ) + jnp.dot(at["first"][...], at["skip"][dim:, :], preferred_element_type=F32)

    first_active = min(s for s in range(4) if roles[s] is not None)
    last_active = max(s for s in range(4) if roles[s] is not None)
    active = (section >= first_active) & (section <= last_active)

    @pl.when(active)
    def _():
        norm[...] = normalise(acc[...], at["gain"][...])
        size = hidden // 2
        for c in range(2):
            cut = pl.ds(c * size, size)
            h = gelu(jnp.dot(norm[...], w1[:, cut], preferred_element_type=F32)).astype(BF16)
            acc[...] += jnp.dot(h, w2[cut, :], preferred_element_type=F32)
        if any(r is not None for r in roles[:3]):
            at["y"][...] = acc[...].astype(BF16)

    if roles[3] is not None:
        part = roles[3]
        totals = at["totals"]

        @pl.when(section == 3)
        def _():
            deep = acc[...].astype(BF16)
            noise = jnp.dot(deep, at["outp"][...], preferred_element_type=F32)
            noise = noise.astype(BF16).astype(F32).reshape(TILE, HALF, noise.shape[-1])
            if part == 0:
                totals[...] = jnp.zeros(totals.shape, F32)
            else:
                totals[...] = at["sums"][...]
            rows = pl.ds(anchor_of(part), TILE)
            totals[rows] = totals[rows] + noise
            if part == 3:
                row = lax.broadcasted_iota(jnp.int32, totals.shape, 0)
                count = jnp.zeros(totals.shape, F32)
                for k in range(4):
                    a = anchor_of(k)
                    count += ((row >= a) & (row < a + TILE)).astype(F32)
                at["final"][...] = (totals[...] / count).astype(BF16)


def per_device(
    latent, anchors, in_proj, pos_embed, section_w1, section_w2, section_gain, skip_w, out_proj
):
    section = lax.axis_index("section")
    slab = lax.axis_index("win")
    sections, slabs = lax.axis_size("section"), lax.axis_size("win")
    height, width, feat = latent.shape
    dim = in_proj.shape[1]
    hidden = section_w1.shape[2]
    tokens = TILE * HALF
    parity = slab % 2
    odd = (slab - 1 + parity) % slabs
    axes = ("section", "win")
    positions = pos_embed.reshape(TILE, 2, HALF, dim)

    def hop(value, *pairs):
        return lax.ppermute(
            value, axes, [(a * slabs + w, b * slabs + w) for a, b in pairs for w in range(slabs)]
        )

    smem = pl.BlockSpec(memory_space=pltpu.SMEM)
    vmem = pl.BlockSpec(memory_space=pltpu.VMEM)
    hbm = pl.BlockSpec(memory_space=pltpu.HBM)

    grid = lax.broadcasted_iota(jnp.int32, (2, slabs), 1)
    mine = anchors[:, 1:2] // STRIDE == grid
    rows = anchors[:, 0:1]
    sums = jnp.sum(jnp.where(mine, rows, 0), axis=0)
    tops = jnp.max(jnp.where(mine, rows, -1), axis=0)
    table = jnp.stack([sums, tops])
    step = 1
    while step < slabs:
        other = lax.ppermute(table, "win", [(w, w ^ step) for w in range(slabs)])
        table = pl.pallas_call(
            join_kernel,
            out_shape=jax.ShapeDtypeStruct(table.shape, table.dtype),
            in_specs=[vmem, vmem],
            out_specs=vmem,
            compiler_params=pltpu.CompilerParams(vmem_limit_bytes=MIB),
        )(table, other)
        step *= 2
    meta = jnp.stack([section, parity, odd]).astype(jnp.int32)

    act = jax.ShapeDtypeStruct((tokens, dim), BF16)
    scratch = [pltpu.VMEM((tokens, dim), BF16), pltpu.VMEM((tokens, dim), F32)]
    chunks = 5
    flops = 4 * tokens * dim * hidden

    def like(a, shape=None):
        return jax.ShapeDtypeStruct(shape or a.shape, a.dtype)

    def held(a, shape=None):
        return pltpu.VMEM(shape or a.shape, a.dtype)

    def pinned(a):
        return pltpu.with_memory_space_constraint(a, pltpu.VMEM)

    y, lat, inp, pos, gain, w1, w2, skip, outp = pl.pallas_call(
        functools.partial(load_kernel, chunks),
        out_shape=[
            act, held(latent), held(in_proj), held(positions), held(section_gain),
            held(section_w1, (dim, hidden)), held(section_w2, (hidden, dim)),
            held(skip_w), held(out_proj),
        ],
        in_specs=[smem] + [hbm] * 8,
        out_specs=[vmem] * 9,
        scratch_shapes=scratch + [pltpu.SemaphoreType.DMA((5 + 2 * chunks + 1,))],
        compiler_params=pltpu.CompilerParams(vmem_limit_bytes=16 * MIB),
        cost_estimate=pl.CostEstimate(flops=flops, bytes_accessed=13 * MIB, transcendentals=0),
    )(
        meta,
        *(
            pltpu.with_memory_space_constraint(a, pltpu.HBM)
            for a in (
                latent, in_proj, positions, section_gain, section_w1, section_w2, skip_w, out_proj
            )
        ),
    )

    lat, inp, pos, gain, w1, w2, skip, outp = map(pinned, (lat, inp, pos, gain, w1, w2, skip, outp))

    def tick(roles, **extra):
        given = dict(
            meta=meta, table=table, gain=gain, w1=w1, w2=w2,
        )
        if roles[0] is not None:
            given.update(lat=lat, inp=inp, pos=pos)
        if roles[3] is not None:
            given.update(skip=skip, outp=outp)
        given.update(extra)
        outs = {}
        if any(r is not None for r in roles[:3]):
            outs["y"] = act
        room = []
        if roles[3] == 3:
            outs["final"] = like(latent)
            room = [pltpu.VMEM(latent.shape, F32)]
        elif roles[3] is not None:
            outs["totals"] = jax.ShapeDtypeStruct(latent.shape, F32)
        names = [*given, *outs, "norm", "acc", *(["totals"] if room else [])]
        results = pl.pallas_call(
            functools.partial(tick_kernel, roles, names, list(outs)),
            out_shape=list(outs.values()),
            in_specs=[smem if k in ("meta", "table") else vmem for k in given],
            out_specs=[vmem] * len(outs),
            scratch_shapes=scratch + room,
            compiler_params=pltpu.CompilerParams(vmem_limit_bytes=16 * MIB),
            cost_estimate=pl.CostEstimate(flops=flops, bytes_accessed=MIB, transcendentals=0),
        )(*given.values())
        return dict(zip(outs, results))

    up, cross = (0, 1), (1, 2)
    near0 = hop(y, (0, 1))
    first0 = hop(y, (0, 3))
    y1 = tick((1, 0, None, None), near=near0)["y"]
    near1 = hop(y1, (0, 1))
    far1 = hop(y1, (1, 2), (0, 3))
    y2 = tick((2, 1, None, None), near=near1)["y"]
    near2 = hop(y2, (0, 1))
    far2 = hop(y2, (1, 2), (0, 3))
    y3 = tick((3, 2, 0, None), near=near2, far=far1)["y"]
    near3 = hop(y3, (0, 1), (2, 3))
    far3 = hop(y3, (1, 2))
    out4 = tick((None, 3, 1, 0), near=near3, far=far2, first=first0)
    near4 = hop(out4["y"], (2, 3))
    far4 = hop(out4["y"], (1, 2))
    first3, _ = lax.optimization_barrier((y3, out4["y"]))
    first3 = hop(first3, (0, 3))
    out5 = tick((None, None, 2, 1), near=near4, far=far3, first=far1, sums=out4["totals"])
    near5 = hop(out5["y"], (2, 3))
    out6 = tick((None, None, 3, 2), near=near5, far=far4, first=far2, sums=out5["totals"])
    near6 = hop(out6["y"], (2, 3))
    final = tick((None, None, None, 3), near=near6, first=first3, sums=out6["totals"])["final"]

    band = height // sections
    parts = [final[s * band : (s + 1) * band] for s in range(sections)]
    sent = [hop(parts[s], (3, s)) for s in range(3)]
    result = parts[3]
    for s in range(3):
        result = jnp.where(section == s, sent[s], result)
    return result


def solution(mesh):
    placed = (
        P(None, "win", None),
        P("win", None),
        P(),
        P(),
        P("section", None, None),
        P("section", None, None),
        P("section", None),
        P(),
        P(),
    )
    return jax.shard_map(
        per_device, mesh=mesh, in_specs=placed, out_specs=P("section", "win", None), check_vma=False
    )
```

```python
import functools

import jax
import jax.numpy as jnp
from jax import lax
from jax.experimental import pallas as pl
from jax.experimental.pallas import tpu as pltpu
from jax.sharding import PartitionSpec as P

TILE = 16
STRIDE = 8
HALF = TILE // 2
ROUNDS = ((16, 2), (1, 4), (4, 4))
MIB = 1 << 20
COST = 16
F32 = jnp.float32
BF16 = jnp.bfloat16


def gelu(v):
    return jax.nn.gelu(v, approximate=True)


def normalise(v, gain):
    factor = lax.rsqrt(jnp.mean(v * v, axis=-1, keepdims=True) + 1e-06)
    return (v * factor * gain).astype(BF16)


def embed_rows(lat, inp, pos, anchors, half):
    width = lat.shape[-1]
    tiles = [
        lat[pl.ds(a, TILE)].astype(F32).reshape(TILE * HALF, width).astype(BF16) for a in anchors
    ]
    place = pos[:, half].astype(F32).reshape(TILE * HALF, pos.shape[-1])
    return [jnp.dot(t, inp[...], preferred_element_type=F32) + place for t in tiles]


def load_kernel(
    chunks, lat_h, inp_h, pos_h, gain_h, w1_h, w2_h,
    y, lat, inp, pos, gain_ref, w1, w2, norm, acc, sems,
):
    section, half = lax.axis_index("section"), lax.rem(lax.axis_index("win"), 2)
    hidden = w1.shape[1]
    size = hidden // chunks
    small = [(lat_h, lat), (inp_h, inp), (pos_h, pos), (gain_h, gain_ref)]
    copies = [pltpu.make_async_copy(a, b, sems.at[k]) for k, (a, b) in enumerate(small)]
    base = len(small)
    for c in range(chunks):
        cut = pl.ds(c * size, size)
        copies.append(pltpu.make_async_copy(w1_h.at[0, :, cut], w1.at[:, cut], sems.at[base + 2 * c]))
        copies.append(pltpu.make_async_copy(w2_h.at[0, cut, :], w2.at[cut, :], sems.at[base + 2 * c + 1]))
    @pl.when(section < 2)
    def _():
        for copy in copies:
            copy.start()
        for copy in copies[:base]:
            copy.wait()

    @pl.when(section == 0)
    def _():
        tokens = TILE * HALF
        for k, v in enumerate(embed_rows(lat, inp, pos, (0, TILE - STRIDE), half)):
            acc[k * tokens : (k + 1) * tokens] = v
        norm[...] = normalise(acc[...], gain_ref[...])

    for c in range(chunks):
        cut = pl.ds(c * size, size)

        @pl.when(section < 2)
        def _():
            copies[base + 2 * c].wait()
            copies[base + 2 * c + 1].wait()

        @pl.when(section == 0)
        def _():
            h = gelu(jnp.dot(norm[...], w1[:, cut], preferred_element_type=F32)).astype(BF16)
            acc[...] += jnp.dot(h, w2[cut, :], preferred_element_type=F32)

    @pl.when(section == 0)
    def _():
        y[...] = acc[...].astype(BF16)

def table_kernel(anchors, out):
    a = anchors[...]
    column = lax.broadcasted_iota(jnp.int32, out.shape, 1) * STRIDE
    upper = lax.broadcasted_iota(jnp.int32, out.shape, 0) == 1
    table = jnp.where(upper, -1, 0)
    for k in range(a.shape[0]):
        row = jnp.broadcast_to(a[k : k + 1, 0:1], out.shape)
        here = jnp.broadcast_to(a[k : k + 1, 1:2], out.shape) == column
        table = jnp.where(here, jnp.where(upper, jnp.maximum(table, row), table + row), table)
    out[...] = table


def join_kernel(*refs):
    *tables, out = refs
    upper = lax.broadcasted_iota(jnp.int32, out.shape, 0) == 1
    total = tables[0][...]
    for table in tables[1:]:
        other = table[...]
        total = jnp.where(upper, jnp.maximum(total, other), total + other)
    out[...] = total


def tick_kernel(roles, outs, names, *refs):
    at = dict(zip(names, refs))
    section, slab = lax.axis_index("section"), lax.axis_index("win")
    parity = lax.rem(slab, 2)
    norm, acc = at["norm"], at["acc"]
    w1, w2 = at.get("new_w1", at["w1"]), at.get("new_w2", at["w2"])
    dim, hidden = w1.shape
    tokens = TILE * HALF

    def anchor_of(part):
        if part < 2:
            return part * STRIDE
        table = at["table"][...]
        slabs = table.shape[1]
        odd = lax.rem(slab + slabs - 1 + parity, slabs)
        here = lax.broadcasted_iota(jnp.int32, table.shape, 1) == odd
        upper = lax.broadcasted_iota(jnp.int32, table.shape, 0) == 1
        top = jnp.sum(jnp.where(here & upper, table, 0))
        return top if part == 2 else jnp.sum(jnp.where(here & ~upper, table, 0)) - top

    def rows_of(s):
        return pl.ds(0, tokens * len(roles[s]))

    def taken(name, s):
        size = tokens * len(roles[s])
        return at[name][pl.ds(tokens * (roles[s][0] % 2) % at[name].shape[0], size)]

    loads = [name for name in names if name.endswith("_h")]
    if loads:
        moves = []
        for k, name in enumerate(loads):
            whole, kept = at[name], at["new_" + name[:-2]]
            moves.append(
                pltpu.make_async_copy(whole.at[0] if whole.ndim > 2 else whole, kept, at["sems"].at[k])
            )

        @pl.when(section >= 2)
        def _():
            for move in moves[:3]:
                move.start()

            @pl.when(section == 3)
            def _():
                for move in moves[3:]:
                    move.start()

            for move in moves[:3]:
                move.wait()

        @pl.when(section == 3)
        def _():
            for move in moves[3:]:
                move.wait()

    if roles[0]:

        @pl.when(section == 0)
        def _():
            half = parity if roles[0][0] < 2 else 1 - parity
            where = [anchor_of(p) for p in roles[0]]
            for k, v in enumerate(embed_rows(at["lat"], at["inp"], at["pos"], where, half)):
                acc[k * tokens : (k + 1) * tokens] = v

    if "pass0" in at:

        @pl.when(section == 0)
        def _():
            at["y"][...] = at["pass0"][...]

    if roles[1]:

        @pl.when(section == 1)
        def _():
            acc[rows_of(1)] = taken("near1", 1).astype(F32)

    if roles[2]:

        @pl.when(section == 2)
        def _():
            acc[rows_of(2)] = taken("far2", 2).astype(F32)

    if roles[3]:

        @pl.when(section == 3)
        def _():
            acc[rows_of(3)] = jnp.dot(
                taken("near3", 3), at["skip"][:dim, :], preferred_element_type=F32
            ) + jnp.dot(taken("first3", 3), at["skip"][dim:, :], preferred_element_type=F32)

    for count in (1, 2):
        busy = [s for s in range(4) if len(roles[s]) == count]
        if not busy:
            continue
        assert busy == list(range(busy[0], busy[-1] + 1))

        @pl.when((section >= busy[0]) & (section <= busy[-1]))
        def _():
            rows = pl.ds(0, tokens * count)
            norm[rows] = normalise(acc[rows], at["gain"][...])
            size = hidden // 2
            for c in range(2):
                cut = pl.ds(c * size, size)
                h = gelu(jnp.dot(norm[rows], w1[:, cut], preferred_element_type=F32)).astype(BF16)
                acc[rows] += jnp.dot(h, w2[cut, :], preferred_element_type=F32)
            for name in sorted({outs[s] for s in busy if s < 3}):
                at[name][...] = acc[rows].astype(BF16)

    if roles[3]:
        totals = at["totals"]

        @pl.when(section == 3)
        def _():
            deep = acc[rows_of(3)].astype(BF16)
            noise = jnp.dot(deep, at["outp"][...], preferred_element_type=F32)
            noise = noise.astype(BF16).astype(F32)
            noise = noise.reshape(len(roles[3]), TILE, HALF, noise.shape[-1])
            if roles[3][0] == 0:
                totals[...] = jnp.zeros(totals.shape, F32)
            else:
                totals[...] = at["sums"][...]
            for k, part in enumerate(roles[3]):
                rows = pl.ds(anchor_of(part), TILE)
                totals[rows] = totals[rows] + noise[k]
            if roles[3][-1] == 3:
                row = lax.broadcasted_iota(jnp.int32, totals.shape, 0)
                count = jnp.zeros(totals.shape, F32)
                for k in range(4):
                    a = anchor_of(k)
                    count += ((row >= a) & (row < a + TILE)).astype(F32)
                at["final"][...] = (totals[...] / count).astype(BF16)


def per_device(
    latent, anchors, in_proj, pos_embed, section_w1, section_w2, section_gain, skip_w, out_proj
):
    section = lax.axis_index("section")
    slab = lax.axis_index("win")
    sections, slabs = lax.axis_size("section"), lax.axis_size("win")
    height, width, feat = latent.shape
    dim = in_proj.shape[1]
    hidden = section_w1.shape[2]
    tokens = TILE * HALF
    axes = ("section", "win")
    positions = pos_embed.reshape(TILE, 2, HALF, dim)

    def hop(value, *pairs):
        return lax.ppermute(
            value, axes, [(a * slabs + w, b * slabs + w) for a, b in pairs for w in range(slabs)]
        )

    def swap(value):
        return hop(value, (0, 1), (1, 0), (2, 3), (3, 2))

    vmem = pl.BlockSpec(memory_space=pltpu.VMEM)
    hbm = pl.BlockSpec(memory_space=pltpu.HBM)
    any_space = pl.BlockSpec(memory_space=pl.ANY)

    def small_call(kernel, *given):
        return pl.pallas_call(
            kernel,
            out_shape=jax.ShapeDtypeStruct((2, slabs), jnp.int32),
            in_specs=[vmem] * len(given),
            out_specs=vmem,
            compiler_params=pltpu.CompilerParams(vmem_limit_bytes=MIB),
        )(*given)

    tables = [small_call(table_kernel, anchors)]
    def join(stride, extent):
        pairs = [
            [(w, w + stride * ((w // stride + k) % extent - w // stride % extent)) for w in range(slabs)]
            for k in range(1, extent)
        ]
        others = [lax.ppermute(tables[-1], "win", p) for p in pairs]
        tables.append(small_call(join_kernel, tables[-1], *others))

    join(*ROUNDS[0])

    chunks = 5

    def act(parts):
        return jax.ShapeDtypeStruct((parts * tokens, dim), BF16)

    def room(parts):
        return [pltpu.VMEM((parts * tokens, dim), BF16), pltpu.VMEM((parts * tokens, dim), F32)]

    def like(a, shape=None):
        return jax.ShapeDtypeStruct(shape or a.shape, a.dtype)

    def held(a, shape=None):
        return pltpu.VMEM(shape or a.shape, a.dtype)

    def pinned(a):
        return pltpu.with_memory_space_constraint(a, pltpu.VMEM)

    y0, lat, inp, pos, gain, w1, w2 = pl.pallas_call(
        functools.partial(load_kernel, chunks),
        out_shape=[
            act(2), held(latent), held(in_proj), held(positions), held(section_gain),
            held(section_w1, (dim, hidden)), held(section_w2, (hidden, dim)),
        ],
        in_specs=[hbm] * 6,
        out_specs=[vmem] * 7,
        scratch_shapes=room(2) + [pltpu.SemaphoreType.DMA((4 + 2 * chunks,))],
        compiler_params=pltpu.CompilerParams(vmem_limit_bytes=16 * MIB),
    )(
        *(
            pltpu.with_memory_space_constraint(a, pltpu.HBM)
            for a in (
                latent, in_proj, positions, section_gain, section_w1, section_w2
            )
        ),
    )

    lat, inp, pos, gain, w1, w2 = map(pinned, (lat, inp, pos, gain, w1, w2))
    held_now = dict(gain=gain, w1=w1, w2=w2)
    last_loads = dict(
        gain_h=section_gain, w1_h=section_w1, w2_h=section_w2, skip_h=skip_w, outp_h=out_proj
    )
    late = {}

    def tick(roles, outs, after=(), load={}, **extra):
        roles = [roles.get(s, ()) for s in range(4)]
        outs = [outs.get(s) for s in range(4)]
        given = {**held_now, **({k: late[k] for k in held_now} if late else {})}
        if any(p >= 2 for p in (*roles[0], *roles[3])):
            given["table"] = tables[-1]
        if roles[0]:
            given.update(lat=lat, inp=inp, pos=pos)
        if roles[3]:
            given.update(late)
        given.update(extra)
        specs = [vmem] * len(given) + [any_space] * len(after)
        if load:
            given.update(
                {k: pltpu.with_memory_space_constraint(a, pltpu.HBM) for k, a in load.items()}
            )
            specs += [hbm] * len(load)
        given.update({f"after{k}": a for k, a in enumerate(after)})
        made = {outs[s]: act(len(roles[s])) for s in range(3) if roles[s]}
        aliases = {}
        scratch = dict(zip(("norm", "acc"), room(max(map(len, roles)))))
        if load:
            made.update({"new_" + k[:-2]: held(a, a.shape[-2:]) for k, a in load.items()})
            aliases = {
                list(given).index(k): list(made).index("new_" + k) for k in held_now
            }
            scratch["sems"] = pltpu.SemaphoreType.DMA((len(load),))
        if roles[3] and roles[3][-1] == 3:
            made["final"] = like(latent)
            scratch["totals"] = pltpu.VMEM(latent.shape, F32)
        elif roles[3]:
            made["totals"] = jax.ShapeDtypeStruct(latent.shape, F32)
        results = pl.pallas_call(
            functools.partial(tick_kernel, roles, outs, [*given, *made, *scratch]),
            out_shape=list(made.values()),
            in_specs=specs,
            out_specs=[vmem] * len(made),
            scratch_shapes=list(scratch.values()),
            input_output_aliases=aliases,
            cost_estimate=pl.CostEstimate(
                flops=COST * sum(map(len, roles)) * 4 * tokens * dim * hidden,
                bytes_accessed=MIB,
                transcendentals=0,
            ),
            compiler_params=pltpu.CompilerParams(vmem_limit_bytes=16 * MIB),
        )(*given.values())
        return dict(zip(made, results))

    y0, _ = lax.optimization_barrier((y0, tables[1]))
    near01 = swap(y0)
    first01 = hop(y0, (0, 3))
    k1 = tick({1: (0, 1)}, {1: "y"}, near1=near01, load=last_loads)
    late.update({name[:-2]: pinned(k1["new_" + name[:-2]]) for name in last_loads})
    far01 = hop(k1["y"], (1, 2))
    tables[1], _ = lax.optimization_barrier((tables[1], k1["y"]))
    for stride, extent in ROUNDS[1:]:
        join(stride, extent)
    f2 = tick({0: (2,)}, {0: "y"}, after=[first01, far01])["y"]
    near2 = swap(f2)
    f3 = tick({0: (3,)}, {0: "y"}, after=[f2])["y"]
    s2 = tick({1: (2,)}, {1: "y"}, near1=near2, pass0=f2, after=[f3])["y"]
    cross2 = hop(s2, (1, 2), (0, 3))
    near3 = swap(f3)
    t01 = tick({2: (0, 1)}, {2: "t"}, far2=far01, after=[s2])["t"]
    third01 = swap(t01)
    s3 = tick({1: (3,)}, {1: "y"}, near1=near3, pass0=f3, after=[t01])["y"]
    cross3 = hop(s3, (1, 2), (0, 3))
    d01 = tick({3: (0, 1)}, {}, near3=third01, first3=first01, after=[s3])["totals"]
    t2 = tick({2: (2,)}, {2: "t"}, far2=cross2, after=[d01])["t"]
    third2 = swap(t2)
    t3 = tick({2: (3,)}, {2: "t"}, far2=cross3, after=[t2])["t"]
    d2 = tick({3: (2,)}, {}, near3=third2, first3=cross2, sums=d01)["totals"]
    t3, _ = lax.optimization_barrier((t3, d2))
    third3 = swap(t3)
    final = tick({3: (3,)}, {}, near3=third3, first3=cross3, sums=d2)["final"]

    band = height // sections
    parts = [final[s * band : (s + 1) * band] for s in range(sections)]
    sent = {s: hop(parts[s], (3, s)) for s in (2, 1, 0)}
    result = parts[3]
    for s in range(3):
        result = jnp.where(section == s, sent[s], result)
    return result


def solution(mesh):
    placed = (
        P(None, "win", None),
        P("win", None),
        P(),
        P(),
        P("section", None, None),
        P("section", None, None),
        P("section", None),
        P(),
        P(),
    )
    return jax.shard_map(
        per_device, mesh=mesh, in_specs=placed, out_specs=P("section", "win", None), check_vma=False
    )
```

```python
import functools

import jax
import jax.numpy as jnp
from jax import lax
from jax.experimental import pallas as pl
from jax.experimental.pallas import tpu as pltpu
from jax.sharding import PartitionSpec as P

TILE = 16
STRIDE = 8
HALF = TILE // 2
ROUNDS = ((16, 2), (1, 4), (4, 4))
MIB = 1 << 20
COST = 16
F32 = jnp.float32
BF16 = jnp.bfloat16


def gelu(v):
    return jax.nn.gelu(v, approximate=True)


def normalise(v, gain):
    factor = lax.rsqrt(jnp.mean(v * v, axis=-1, keepdims=True) + 1e-06)
    return (v * factor * gain).astype(BF16)


def embed_rows(lat, inp, pos, anchors, half):
    width = lat.shape[-1]
    tiles = [
        lat[pl.ds(a, TILE)].astype(F32).reshape(TILE * HALF, width).astype(BF16) for a in anchors
    ]
    place = pos[:, half].astype(F32).reshape(TILE * HALF, pos.shape[-1])
    return [jnp.dot(t, inp[...], preferred_element_type=F32) + place for t in tiles]


def load_kernel(
    chunks, lat_h, inp_h, pos_h, gain_h, w1_h, w2_h,
    y, lat, inp, pos, gain_ref, w1, w2, norm, acc, sems,
):
    section, half = lax.axis_index("section"), lax.rem(lax.axis_index("win"), 2)
    hidden = w1.shape[1]
    size = hidden // chunks
    small = [(lat_h, lat), (inp_h, inp), (pos_h, pos), (gain_h, gain_ref)]
    copies = [pltpu.make_async_copy(a, b, sems.at[k]) for k, (a, b) in enumerate(small)]
    base = len(small)
    for c in range(chunks):
        cut = pl.ds(c * size, size)
        copies.append(pltpu.make_async_copy(w1_h.at[0, :, cut], w1.at[:, cut], sems.at[base + 2 * c]))
        copies.append(pltpu.make_async_copy(w2_h.at[0, cut, :], w2.at[cut, :], sems.at[base + 2 * c + 1]))
    @pl.when(section < 2)
    def _():
        for copy in copies:
            copy.start()
        for copy in copies[:base]:
            copy.wait()

    @pl.when(section == 0)
    def _():
        tokens = TILE * HALF
        for k, v in enumerate(embed_rows(lat, inp, pos, (0, TILE - STRIDE), half)):
            acc[k * tokens : (k + 1) * tokens] = v
        norm[...] = normalise(acc[...], gain_ref[...])

    for c in range(chunks):
        cut = pl.ds(c * size, size)

        @pl.when(section < 2)
        def _():
            copies[base + 2 * c].wait()
            copies[base + 2 * c + 1].wait()

        @pl.when(section == 0)
        def _():
            h = gelu(jnp.dot(norm[...], w1[:, cut], preferred_element_type=F32)).astype(BF16)
            acc[...] += jnp.dot(h, w2[cut, :], preferred_element_type=F32)

    @pl.when(section == 0)
    def _():
        y[...] = acc[...].astype(BF16)

def table_kernel(anchors, out):
    a = anchors[...]
    column = lax.broadcasted_iota(jnp.int32, out.shape, 1) * STRIDE
    upper = lax.broadcasted_iota(jnp.int32, out.shape, 0) == 1
    table = jnp.where(upper, -1, 0)
    for k in range(a.shape[0]):
        row = jnp.broadcast_to(a[k : k + 1, 0:1], out.shape)
        here = jnp.broadcast_to(a[k : k + 1, 1:2], out.shape) == column
        table = jnp.where(here, jnp.where(upper, jnp.maximum(table, row), table + row), table)
    out[...] = table


def join_kernel(*refs):
    *tables, out = refs
    upper = lax.broadcasted_iota(jnp.int32, out.shape, 0) == 1
    total = tables[0][...]
    for table in tables[1:]:
        other = table[...]
        total = jnp.where(upper, jnp.maximum(total, other), total + other)
    out[...] = total


def tick_kernel(roles, outs, names, *refs):
    at = dict(zip(names, refs))
    section, slab = lax.axis_index("section"), lax.axis_index("win")
    parity = lax.rem(slab, 2)
    norm, acc = at["norm"], at["acc"]
    w1, w2 = at.get("new_w1", at["w1"]), at.get("new_w2", at["w2"])
    dim, hidden = w1.shape
    tokens = TILE * HALF

    def anchor_of(part):
        if part < 2:
            return part * STRIDE
        table = at["table"][...]
        slabs = table.shape[1]
        odd = lax.rem(slab + slabs - 1 + parity, slabs)
        here = lax.broadcasted_iota(jnp.int32, table.shape, 1) == odd
        upper = lax.broadcasted_iota(jnp.int32, table.shape, 0) == 1
        top = jnp.sum(jnp.where(here & upper, table, 0))
        return top if part == 2 else jnp.sum(jnp.where(here & ~upper, table, 0)) - top

    def rows_of(s):
        return pl.ds(0, tokens * len(roles[s]))

    def taken(name, s):
        size = tokens * len(roles[s])
        return at[name][pl.ds(tokens * (roles[s][0] % 2) % at[name].shape[0], size)]

    loads = [name for name in names if name.endswith("_h")]
    if loads:
        moves = []
        for k, name in enumerate(loads):
            whole, kept = at[name], at["new_" + name[:-2]]
            moves.append(
                pltpu.make_async_copy(whole.at[0] if whole.ndim > 2 else whole, kept, at["sems"].at[k])
            )

        @pl.when(section >= 2)
        def _():
            for move in moves[:3]:
                move.start()

            @pl.when(section == 3)
            def _():
                for move in moves[3:]:
                    move.start()

            for move in moves[:3]:
                move.wait()

        @pl.when(section == 3)
        def _():
            for move in moves[3:]:
                move.wait()

    if roles[0]:

        @pl.when(section == 0)
        def _():
            half = parity if roles[0][0] < 2 else 1 - parity
            where = [anchor_of(p) for p in roles[0]]
            for k, v in enumerate(embed_rows(at["lat"], at["inp"], at["pos"], where, half)):
                acc[k * tokens : (k + 1) * tokens] = v

    if "pass0" in at:

        @pl.when(section == 0)
        def _():
            at["y"][...] = at["pass0"][...]

    if roles[1]:

        @pl.when(section == 1)
        def _():
            acc[rows_of(1)] = taken("near1", 1).astype(F32)

    if roles[2]:

        @pl.when(section == 2)
        def _():
            acc[rows_of(2)] = taken("far2", 2).astype(F32)

    if roles[3]:

        @pl.when(section == 3)
        def _():
            acc[rows_of(3)] = jnp.dot(
                taken("near3", 3), at["skip"][:dim, :], preferred_element_type=F32
            ) + jnp.dot(taken("first3", 3), at["skip"][dim:, :], preferred_element_type=F32)

    for count in (1, 2):
        busy = [s for s in range(4) if len(roles[s]) == count]
        if not busy:
            continue
        assert busy == list(range(busy[0], busy[-1] + 1))

        @pl.when((section >= busy[0]) & (section <= busy[-1]))
        def _():
            rows = pl.ds(0, tokens * count)
            norm[rows] = normalise(acc[rows], at["gain"][...])
            size = hidden // 2

            def piece(c):
                cut = pl.ds(c * size, size)
                h = gelu(jnp.dot(norm[rows], w1[:, cut], preferred_element_type=F32)).astype(BF16)
                acc[rows] += jnp.dot(h, w2[cut, :], preferred_element_type=F32)

            if count == 1:
                piece(0)
                piece(1)
            else:
                pl.loop(0, 2)(piece)
            for name in sorted({outs[s] for s in busy if s < 3}):
                at[name][...] = acc[rows].astype(BF16)

    if roles[3]:
        totals = at["totals"]

        @pl.when(section == 3)
        def _():
            deep = acc[rows_of(3)].astype(BF16)
            noise = jnp.dot(deep, at["outp"][...], preferred_element_type=F32)
            noise = noise.astype(BF16).astype(F32)
            noise = noise.reshape(len(roles[3]), TILE, HALF, noise.shape[-1])
            if roles[3][0] == 0:
                totals[...] = jnp.zeros(totals.shape, F32)
            else:
                totals[...] = at["sums"][...]
            for k, part in enumerate(roles[3]):
                rows = pl.ds(anchor_of(part), TILE)
                totals[rows] = totals[rows] + noise[k]
            if roles[3][-1] == 3:
                row = lax.broadcasted_iota(jnp.int32, totals.shape, 0)
                count = jnp.zeros(totals.shape, F32)
                for k in range(4):
                    a = anchor_of(k)
                    count += ((row >= a) & (row < a + TILE)).astype(F32)
                band = totals.shape[0] // 4
                for k in range(4):
                    rows = slice(k * band, (k + 1) * band)
                    at[f"band{k}"][...] = (totals[rows] / count[rows]).astype(BF16)


def per_device(
    latent, anchors, in_proj, pos_embed, section_w1, section_w2, section_gain, skip_w, out_proj
):
    section = lax.axis_index("section")
    slab = lax.axis_index("win")
    sections, slabs = lax.axis_size("section"), lax.axis_size("win")
    height, width, feat = latent.shape
    dim = in_proj.shape[1]
    hidden = section_w1.shape[2]
    tokens = TILE * HALF
    axes = ("section", "win")
    positions = pos_embed.reshape(TILE, 2, HALF, dim)

    def hop(value, *pairs):
        return lax.ppermute(
            value, axes, [(a * slabs + w, b * slabs + w) for a, b in pairs for w in range(slabs)]
        )

    def swap(value):
        return hop(value, (0, 1), (1, 0), (2, 3), (3, 2))

    vmem = pl.BlockSpec(memory_space=pltpu.VMEM)
    hbm = pl.BlockSpec(memory_space=pltpu.HBM)
    any_space = pl.BlockSpec(memory_space=pl.ANY)

    def small_call(kernel, *given):
        return pl.pallas_call(
            kernel,
            out_shape=jax.ShapeDtypeStruct((2, slabs), jnp.int32),
            in_specs=[vmem] * len(given),
            out_specs=vmem,
            compiler_params=pltpu.CompilerParams(vmem_limit_bytes=MIB),
        )(*given)

    tables = [small_call(table_kernel, anchors)]
    def join(stride, extent):
        pairs = [
            [(w, w + stride * ((w // stride + k) % extent - w // stride % extent)) for w in range(slabs)]
            for k in range(1, extent)
        ]
        others = [lax.ppermute(tables[-1], "win", p) for p in pairs]
        tables.append(small_call(join_kernel, tables[-1], *others))

    join(*ROUNDS[0])

    chunks = 5

    def act(parts):
        return jax.ShapeDtypeStruct((parts * tokens, dim), BF16)

    def room(parts):
        return [pltpu.VMEM((parts * tokens, dim), BF16), pltpu.VMEM((parts * tokens, dim), F32)]

    def like(a, shape=None):
        return jax.ShapeDtypeStruct(shape or a.shape, a.dtype)

    def held(a, shape=None):
        return pltpu.VMEM(shape or a.shape, a.dtype)

    def pinned(a):
        return pltpu.with_memory_space_constraint(a, pltpu.VMEM)

    y0, lat, inp, pos, gain, w1, w2 = pl.pallas_call(
        functools.partial(load_kernel, chunks),
        out_shape=[
            act(2), held(latent), held(in_proj), held(positions), held(section_gain),
            held(section_w1, (dim, hidden)), held(section_w2, (hidden, dim)),
        ],
        in_specs=[hbm] * 6,
        out_specs=[vmem] * 7,
        scratch_shapes=room(2) + [pltpu.SemaphoreType.DMA((4 + 2 * chunks,))],
        compiler_params=pltpu.CompilerParams(vmem_limit_bytes=16 * MIB),
    )(
        *(
            pltpu.with_memory_space_constraint(a, pltpu.HBM)
            for a in (
                latent, in_proj, positions, section_gain, section_w1, section_w2
            )
        ),
    )

    lat, inp, pos, gain, w1, w2 = map(pinned, (lat, inp, pos, gain, w1, w2))
    held_now = dict(gain=gain, w1=w1, w2=w2)
    last_loads = dict(
        gain_h=section_gain, w1_h=section_w1, w2_h=section_w2, skip_h=skip_w, outp_h=out_proj
    )
    late = {}

    def tick(roles, outs, after=(), load={}, **extra):
        roles = [roles.get(s, ()) for s in range(4)]
        outs = [outs.get(s) for s in range(4)]
        given = {**held_now, **({k: late[k] for k in held_now} if late else {})}
        if any(p >= 2 for p in (*roles[0], *roles[3])):
            given["table"] = tables[-1]
        if roles[0]:
            given.update(lat=lat, inp=inp, pos=pos)
        if roles[3]:
            given.update(late)
        given.update(extra)
        specs = [vmem] * len(given) + [any_space] * len(after)
        if load:
            given.update(
                {k: pltpu.with_memory_space_constraint(a, pltpu.HBM) for k, a in load.items()}
            )
            specs += [hbm] * len(load)
        given.update({f"after{k}": a for k, a in enumerate(after)})
        made = {outs[s]: act(len(roles[s])) for s in range(3) if roles[s]}
        aliases = {}
        scratch = dict(zip(("norm", "acc"), room(max(map(len, roles)))))
        if load:
            made.update({"new_" + k[:-2]: held(a, a.shape[-2:]) for k, a in load.items()})
            aliases = {
                list(given).index(k): list(made).index("new_" + k) for k in held_now
            }
            scratch["sems"] = pltpu.SemaphoreType.DMA((len(load),))
        if roles[3] and roles[3][-1] == 3:
            for k in range(sections):
                made[f"band{k}"] = like(latent, (height // sections, *latent.shape[1:]))
            scratch["totals"] = pltpu.VMEM(latent.shape, F32)
        elif roles[3]:
            made["totals"] = jax.ShapeDtypeStruct(latent.shape, F32)
        results = pl.pallas_call(
            functools.partial(tick_kernel, roles, outs, [*given, *made, *scratch]),
            out_shape=list(made.values()),
            in_specs=specs,
            out_specs=[vmem] * len(made),
            scratch_shapes=list(scratch.values()),
            input_output_aliases=aliases,
            cost_estimate=pl.CostEstimate(
                flops=COST * sum(map(len, roles)) * 4 * tokens * dim * hidden,
                bytes_accessed=MIB,
                transcendentals=0,
            ),
            compiler_params=pltpu.CompilerParams(vmem_limit_bytes=16 * MIB),
        )(*given.values())
        return dict(zip(made, results))

    y0, _ = lax.optimization_barrier((y0, tables[1]))
    near01 = swap(y0)
    first01 = hop(y0, (0, 3))
    k1 = tick({1: (0, 1)}, {1: "y"}, near1=near01, load=last_loads)
    late.update({name[:-2]: pinned(k1["new_" + name[:-2]]) for name in last_loads})
    far01 = hop(k1["y"], (1, 2))
    tables[1], _ = lax.optimization_barrier((tables[1], k1["y"]))
    for stride, extent in ROUNDS[1:]:
        join(stride, extent)
    f2 = tick({0: (2,)}, {0: "y"}, after=[first01, far01])["y"]
    near2 = swap(f2)
    f3 = tick({0: (3,)}, {0: "y"}, after=[f2])["y"]
    s2 = tick({1: (2,)}, {1: "y"}, near1=near2, pass0=f2, after=[f3])["y"]
    cross2 = hop(s2, (1, 2), (0, 3))
    near3 = swap(f3)
    t01 = tick({2: (0, 1)}, {2: "t"}, far2=far01, after=[s2])["t"]
    third01 = swap(t01)
    s3 = tick({1: (3,)}, {1: "y"}, near1=near3, pass0=f3, after=[t01])["y"]
    cross3 = hop(s3, (1, 2), (0, 3))
    d01 = tick({3: (0, 1)}, {}, near3=third01, first3=first01, after=[s3])["totals"]
    t2 = tick({2: (2,)}, {2: "t"}, far2=cross2, after=[d01])["t"]
    third2 = swap(t2)
    t3 = tick({2: (3,)}, {2: "t"}, far2=cross3, after=[t2])["t"]
    d2 = tick({3: (2,)}, {}, near3=third2, first3=cross2, sums=d01)["totals"]
    t3, _ = lax.optimization_barrier((t3, d2))
    third3 = swap(t3)
    bands = tick({3: (3,)}, {}, near3=third3, first3=cross3, sums=d2)
    sent = [hop(bands[f"band{s}"], (3, s)) for s in range(3)]
    result = bands["band3"]
    for s in range(3):
        result = jnp.where(section == s, sent[s], result)
    return result


def solution(mesh):
    placed = (
        P(None, "win", None),
        P("win", None),
        P(),
        P(),
        P("section", None, None),
        P("section", None, None),
        P("section", None),
        P(),
        P(),
    )
    return jax.shard_map(
        per_device, mesh=mesh, in_specs=placed, out_specs=P("section", "win", None), check_vma=False
    )
```

```python
import functools

import jax
import jax.numpy as jnp
from jax import lax
from jax.experimental import pallas as pl
from jax.experimental.pallas import tpu as pltpu
from jax.sharding import PartitionSpec as P

TILE = 16
STRIDE = 8
HALF = TILE // 2
ROUNDS = ((16, 2), (1, 4), (4, 4))
MIB = 1 << 20
COST = 8
F32 = jnp.float32
BF16 = jnp.bfloat16


def gelu(v):
    return jax.nn.gelu(v, approximate=True)


def normalise(v, gain):
    factor = lax.rsqrt(jnp.mean(v * v, axis=-1, keepdims=True) + 1e-06)
    return (v * factor * gain).astype(BF16)


def embed_rows(lat, inp, pos, anchors, half):
    width = lat.shape[-1]
    tiles = [
        lat[pl.ds(a, TILE)].astype(F32).reshape(TILE * HALF, width).astype(BF16) for a in anchors
    ]
    place = pos[:, half].astype(F32).reshape(TILE * HALF, pos.shape[-1])
    return [jnp.dot(t, inp[...], preferred_element_type=F32) + place for t in tiles]


def load_kernel(
    chunks, lat_h, inp_h, pos_h, gain_h, w1_h, w2_h,
    y, lat, inp, pos, gain_ref, w1, w2, norm, acc, sems,
):
    section, half = lax.axis_index("section"), lax.rem(lax.axis_index("win"), 2)
    hidden = w1.shape[1]
    size = hidden // chunks
    small = [(lat_h, lat), (inp_h, inp), (pos_h, pos), (gain_h, gain_ref)]
    copies = [pltpu.make_async_copy(a, b, sems.at[k]) for k, (a, b) in enumerate(small)]
    base = len(small)
    for c in range(chunks):
        cut = pl.ds(c * size, size)
        copies.append(pltpu.make_async_copy(w1_h.at[0, :, cut], w1.at[:, cut], sems.at[base + 2 * c]))
        copies.append(pltpu.make_async_copy(w2_h.at[0, cut, :], w2.at[cut, :], sems.at[base + 2 * c + 1]))
    @pl.when(section < 2)
    def _():
        for copy in copies:
            copy.start()
        for copy in copies[:base]:
            copy.wait()

    @pl.when(section == 0)
    def _():
        tokens = TILE * HALF
        for k, v in enumerate(embed_rows(lat, inp, pos, (0, TILE - STRIDE), half)):
            acc[k * tokens : (k + 1) * tokens] = v
        norm[...] = normalise(acc[...], gain_ref[...])

    @pl.when(section < 2)
    def _():
        @pl.loop(0, chunks)
        def _(c):
            cut = pl.ds(pl.multiple_of(c * size, size), size)
            pltpu.make_async_copy(w1_h.at[0, :, cut], w1.at[:, cut], sems.at[base + 2 * c]).wait()
            pltpu.make_async_copy(w2_h.at[0, cut, :], w2.at[cut, :], sems.at[base + 2 * c + 1]).wait()

            @pl.when(section == 0)
            def _():
                h = gelu(jnp.dot(norm[...], w1[:, cut], preferred_element_type=F32)).astype(BF16)
                acc[...] += jnp.dot(h, w2[cut, :], preferred_element_type=F32)

    @pl.when(section == 0)
    def _():
        y[...] = acc[...].astype(BF16)

def table_kernel(anchors, out):
    a = anchors[...]
    column = lax.broadcasted_iota(jnp.int32, out.shape, 1) * STRIDE
    upper = lax.broadcasted_iota(jnp.int32, out.shape, 0) == 1
    table = jnp.where(upper, -1, 0)
    for k in range(a.shape[0]):
        row = jnp.broadcast_to(a[k : k + 1, 0:1], out.shape)
        here = jnp.broadcast_to(a[k : k + 1, 1:2], out.shape) == column
        table = jnp.where(here, jnp.where(upper, jnp.maximum(table, row), table + row), table)
    out[...] = table


def join_kernel(*refs):
    *tables, out = refs
    upper = lax.broadcasted_iota(jnp.int32, out.shape, 0) == 1
    total = tables[0][...]
    for table in tables[1:]:
        other = table[...]
        total = jnp.where(upper, jnp.maximum(total, other), total + other)
    out[...] = total


def tick_kernel(roles, outs, names, *refs):
    at = dict(zip(names, refs))
    section, slab = lax.axis_index("section"), lax.axis_index("win")
    parity = lax.rem(slab, 2)
    norm, acc = at["norm"], at["acc"]
    w1, w2 = at.get("new_w1", at["w1"]), at.get("new_w2", at["w2"])
    dim, hidden = w1.shape
    tokens = TILE * HALF

    def anchor_of(part):
        if part < 2:
            return part * STRIDE
        table = at["table"][...]
        slabs = table.shape[1]
        odd = lax.rem(slab + slabs - 1 + parity, slabs)
        here = lax.broadcasted_iota(jnp.int32, table.shape, 1) == odd
        upper = lax.broadcasted_iota(jnp.int32, table.shape, 0) == 1
        top = jnp.sum(jnp.where(here & upper, table, 0))
        return top if part == 2 else jnp.sum(jnp.where(here & ~upper, table, 0)) - top

    def rows_of(s):
        return pl.ds(0, tokens * len(roles[s]))

    def taken(name, s):
        size = tokens * len(roles[s])
        return at[name][pl.ds(tokens * (roles[s][0] % 2) % at[name].shape[0], size)]

    loads = [name for name in names if name.endswith("_h")]
    if loads:
        moves = []
        for k, name in enumerate(loads):
            whole, kept = at[name], at["new_" + name[:-2]]
            moves.append(
                pltpu.make_async_copy(whole.at[0] if whole.ndim > 2 else whole, kept, at["sems"].at[k])
            )

        @pl.when(section >= 2)
        def _():
            for move in moves[:3]:
                move.start()

            @pl.when(section == 3)
            def _():
                for move in moves[3:]:
                    move.start()

            for move in moves[:3]:
                move.wait()

        @pl.when(section == 3)
        def _():
            for move in moves[3:]:
                move.wait()

    if roles[0]:

        @pl.when(section == 0)
        def _():
            half = parity if roles[0][0] < 2 else 1 - parity
            where = [anchor_of(p) for p in roles[0]]
            for k, v in enumerate(embed_rows(at["lat"], at["inp"], at["pos"], where, half)):
                acc[k * tokens : (k + 1) * tokens] = v

    if roles[1]:

        @pl.when(section == 1)
        def _():
            acc[rows_of(1)] = taken("near1", 1).astype(F32)

    if roles[2]:

        @pl.when(section == 2)
        def _():
            acc[rows_of(2)] = taken("far2", 2).astype(F32)

    if roles[3]:

        @pl.when(section == 3)
        def _():
            acc[rows_of(3)] = jnp.dot(
                taken("near3", 3), at["skip"][:dim, :], preferred_element_type=F32
            ) + jnp.dot(taken("first3", 3), at["skip"][dim:, :], preferred_element_type=F32)

    for count in (1, 2):
        busy = [s for s in range(4) if len(roles[s]) == count]
        if not busy:
            continue
        assert busy == list(range(busy[0], busy[-1] + 1))

        @pl.when((section >= busy[0]) & (section <= busy[-1]))
        def _():
            rows = pl.ds(0, tokens * count)
            norm[rows] = normalise(acc[rows], at["gain"][...])
            size = hidden // 2

            def piece(c):
                cut = pl.ds(c * size, size)
                h = gelu(jnp.dot(norm[rows], w1[:, cut], preferred_element_type=F32)).astype(BF16)
                acc[rows] += jnp.dot(h, w2[cut, :], preferred_element_type=F32)

            if count == 1:
                piece(0)
                piece(1)
            else:
                pl.loop(0, 2)(piece)
            for name in sorted({outs[s] for s in busy if s < 3}):
                at[name][...] = acc[rows].astype(BF16)

    if roles[3]:
        totals = at["totals"]

        @pl.when(section == 3)
        def _():
            deep = acc[rows_of(3)].astype(BF16)
            noise = jnp.dot(deep, at["outp"][...], preferred_element_type=F32)
            noise = noise.astype(BF16).astype(F32)
            noise = noise.reshape(len(roles[3]), TILE, HALF, noise.shape[-1])
            if roles[3][0] == 0:
                totals[...] = jnp.zeros(totals.shape, F32)
            else:
                totals[...] = at["sums"][...]
            for k, part in enumerate(roles[3]):
                rows = pl.ds(anchor_of(part), TILE)
                totals[rows] = totals[rows] + noise[k]
            if roles[3][-1] == 3:
                row = lax.broadcasted_iota(jnp.int32, totals.shape, 0)
                count = jnp.zeros(totals.shape, F32)
                for k in range(4):
                    a = anchor_of(k)
                    count += ((row >= a) & (row < a + TILE)).astype(F32)
                band = totals.shape[0] // 4
                for k in range(4):
                    rows = slice(k * band, (k + 1) * band)
                    at[f"band{k}"][...] = (totals[rows] / count[rows]).astype(BF16)


def per_device(
    latent, anchors, in_proj, pos_embed, section_w1, section_w2, section_gain, skip_w, out_proj
):
    section = lax.axis_index("section")
    slab = lax.axis_index("win")
    sections, slabs = lax.axis_size("section"), lax.axis_size("win")
    height, width, feat = latent.shape
    dim = in_proj.shape[1]
    hidden = section_w1.shape[2]
    tokens = TILE * HALF
    axes = ("section", "win")
    positions = pos_embed.reshape(TILE, 2, HALF, dim)

    def hop(value, *pairs):
        return lax.ppermute(
            value, axes, [(a * slabs + w, b * slabs + w) for a, b in pairs for w in range(slabs)]
        )

    def swap(value):
        return hop(value, (0, 1), (1, 0), (2, 3), (3, 2))

    vmem = pl.BlockSpec(memory_space=pltpu.VMEM)
    hbm = pl.BlockSpec(memory_space=pltpu.HBM)
    any_space = pl.BlockSpec(memory_space=pl.ANY)

    def small_call(kernel, *given):
        return pl.pallas_call(
            kernel,
            out_shape=jax.ShapeDtypeStruct((2, slabs), jnp.int32),
            in_specs=[vmem] * len(given),
            out_specs=vmem,
            compiler_params=pltpu.CompilerParams(vmem_limit_bytes=MIB),
        )(*given)

    tables = [small_call(table_kernel, anchors)]
    def join(stride, extent):
        pairs = [
            [(w, w + stride * ((w // stride + k) % extent - w // stride % extent)) for w in range(slabs)]
            for k in range(1, extent)
        ]
        others = [lax.ppermute(tables[-1], "win", p) for p in pairs]
        tables.append(small_call(join_kernel, tables[-1], *others))

    join(*ROUNDS[0])

    chunks = 5
    flops = 4 * tokens * dim * hidden

    def act(parts):
        return pltpu.VMEM((parts * tokens, dim), BF16)

    def room(parts):
        return [pltpu.VMEM((parts * tokens, dim), BF16), pltpu.VMEM((parts * tokens, dim), F32)]

    def like(a, shape=None):
        return jax.ShapeDtypeStruct(shape or a.shape, a.dtype)

    def held(a, shape=None):
        return pltpu.VMEM(shape or a.shape, a.dtype)

    def pinned(a):
        return pltpu.with_memory_space_constraint(a, pltpu.VMEM)

    y0, lat, inp, pos, gain, w1, w2 = pl.pallas_call(
        functools.partial(load_kernel, chunks),
        out_shape=[
            act(2), held(latent), held(in_proj), held(positions), held(section_gain),
            held(section_w1, (dim, hidden)), held(section_w2, (hidden, dim)),
        ],
        in_specs=[hbm] * 6,
        out_specs=[vmem] * 7,
        scratch_shapes=room(2) + [pltpu.SemaphoreType.DMA((4 + 2 * chunks,))],
        compiler_params=pltpu.CompilerParams(vmem_limit_bytes=16 * MIB),
    )(
        *(
            pltpu.with_memory_space_constraint(a, pltpu.HBM)
            for a in (
                latent, in_proj, positions, section_gain, section_w1, section_w2
            )
        ),
    )

    lat, inp, pos, gain, w1, w2 = map(pinned, (lat, inp, pos, gain, w1, w2))
    held_now = dict(gain=gain, w1=w1, w2=w2)
    last_loads = dict(
        gain_h=section_gain, w1_h=section_w1, w2_h=section_w2, skip_h=skip_w, outp_h=out_proj
    )
    late = {}

    def tick(roles, outs, after=(), load={}, **extra):
        roles = [roles.get(s, ()) for s in range(4)]
        outs = [outs.get(s) for s in range(4)]
        given = {**held_now, **({k: late[k] for k in held_now} if late else {})}
        if any(p >= 2 for p in (*roles[0], *roles[3])):
            given["table"] = tables[-1]
        if roles[0]:
            given.update(lat=lat, inp=inp, pos=pos)
        if roles[3]:
            given.update(late)
        given.update({k: pinned(a) for k, a in extra.items()})
        specs = [vmem] * len(given) + [any_space] * len(after)
        if load:
            given.update(
                {k: pltpu.with_memory_space_constraint(a, pltpu.HBM) for k, a in load.items()}
            )
            specs += [hbm] * len(load)
        given.update({f"after{k}": a for k, a in enumerate(after)})
        made = {outs[s]: act(len(roles[s])) for s in range(3) if roles[s]}
        aliases = {}
        scratch = dict(zip(("norm", "acc"), room(max(map(len, roles)))))
        if load:
            made.update({"new_" + k[:-2]: held(a, a.shape[-2:]) for k, a in load.items()})
            aliases = {
                list(given).index(k): list(made).index("new_" + k) for k in held_now
            }
            scratch["sems"] = pltpu.SemaphoreType.DMA((len(load),))
        if roles[3] and roles[3][-1] == 3:
            for k in range(sections):
                made[f"band{k}"] = like(latent, (height // sections, *latent.shape[1:]))
            scratch["totals"] = pltpu.VMEM(latent.shape, F32)
        elif roles[3]:
            made["totals"] = pltpu.VMEM(latent.shape, F32)
        results = pl.pallas_call(
            functools.partial(tick_kernel, roles, outs, [*given, *made, *scratch]),
            out_shape=list(made.values()),
            in_specs=specs,
            out_specs=[vmem] * len(made),
            scratch_shapes=list(scratch.values()),
            input_output_aliases=aliases,
            cost_estimate=pl.CostEstimate(
                flops=COST * sum(map(len, roles)) * flops,
                bytes_accessed=MIB,
                transcendentals=0,
            ),
            compiler_params=pltpu.CompilerParams(vmem_limit_bytes=16 * MIB),
        )(*given.values())
        return dict(zip(made, results))

    y0, _ = lax.optimization_barrier((y0, tables[1]))
    near01 = swap(y0)
    first01 = hop(y0, (0, 3))
    k1 = tick({1: (0, 1)}, {1: "y"}, near1=near01, load=last_loads)
    late.update({name[:-2]: pinned(k1["new_" + name[:-2]]) for name in last_loads})
    far01 = hop(k1["y"], (1, 2))
    tables[1], _ = lax.optimization_barrier((tables[1], k1["y"]))
    for stride, extent in ROUNDS[1:]:
        join(stride, extent)
    f2 = tick({0: (2,)}, {0: "y"}, after=[first01, far01])["y"]
    near2 = hop(f2, (0, 1))
    first2 = hop(f2, (0, 3))
    s2 = tick({1: (2,)}, {1: "y"}, near1=near2)["y"]
    far2 = hop(s2, (1, 2))
    f3 = tick({0: (3,)}, {0: "y"}, after=[s2])["y"]
    near3 = swap(f3)
    first3 = hop(f3, (0, 3))
    t01 = tick({2: (0, 1)}, {2: "t"}, far2=far01, after=[f3])["t"]
    third01 = swap(t01)
    s3 = tick({1: (3,)}, {1: "y"}, near1=near3, after=[t01])["y"]
    far3 = hop(s3, (1, 2))
    d01 = tick({3: (0, 1)}, {}, near3=third01, first3=first01, after=[s3])["totals"]
    t2 = tick({2: (2,)}, {2: "t"}, far2=far2, after=[d01])["t"]
    third2 = swap(t2)
    t3 = tick({2: (3,)}, {2: "t"}, far2=far3, after=[t2])["t"]
    d2 = tick({3: (2,)}, {}, near3=third2, first3=first2, sums=d01)["totals"]
    t3, _ = lax.optimization_barrier((t3, d2))
    third3 = swap(t3)
    bands = tick({3: (3,)}, {}, near3=third3, first3=first3, sums=d2)
    sent = [hop(a, (3, s)) for s, a in enumerate(bands[f"band{k}"] for k in range(3))]
    result = bands["band3"]
    for s in range(3):
        result = jnp.where(section == s, sent[s], result)
    return result


def solution(mesh):
    placed = (
        P(None, "win", None),
        P("win", None),
        P(),
        P(),
        P("section", None, None),
        P("section", None, None),
        P("section", None),
        P(),
        P(),
    )
    return jax.shard_map(
        per_device, mesh=mesh, in_specs=placed, out_specs=P("section", "win", None), check_vma=False
    )
```

```python
import functools

import jax
import jax.numpy as jnp
from jax import lax
from jax.experimental import pallas as pl
from jax.experimental.pallas import tpu as pltpu
from jax.sharding import PartitionSpec as P

TILE = 16
STRIDE = 8
HALF = TILE // 2
ROUNDS = ((16, 2), (1, 4), (4, 4))
MIB = 1 << 20
COST = 8
F32 = jnp.float32
BF16 = jnp.bfloat16


def gelu(v):
    return jax.nn.gelu(v, approximate=True)


def normalise(v, gain):
    factor = lax.rsqrt(jnp.mean(v * v, axis=-1, keepdims=True) + 1e-06)
    return (v * factor * gain).astype(BF16)


def embed_rows(lat, inp, pos, anchors, half):
    width = lat.shape[-1]
    tiles = [
        lat[pl.ds(a, TILE)].astype(F32).reshape(TILE * HALF, width).astype(BF16) for a in anchors
    ]
    place = pos[:, half].astype(F32).reshape(TILE * HALF, pos.shape[-1])
    return [jnp.dot(t, inp[...], preferred_element_type=F32) + place for t in tiles]


def load_kernel(
    chunks, lat_h, inp_h, pos_h, gain_h, w1_h, w2_h,
    y, lat, inp, pos, gain_ref, w1, w2, norm, acc, sems,
):
    section, half = lax.axis_index("section"), lax.rem(lax.axis_index("win"), 2)
    hidden = w1.shape[1]
    size = hidden // chunks
    small = [(lat_h, lat), (inp_h, inp), (pos_h, pos), (gain_h, gain_ref)]
    copies = [pltpu.make_async_copy(a, b, sems.at[k]) for k, (a, b) in enumerate(small)]
    base = len(small)
    for c in range(chunks):
        cut = pl.ds(c * size, size)
        copies.append(pltpu.make_async_copy(w1_h.at[0, :, cut], w1.at[:, cut], sems.at[base + 2 * c]))
        copies.append(pltpu.make_async_copy(w2_h.at[0, cut, :], w2.at[cut, :], sems.at[base + 2 * c + 1]))
    @pl.when(section < 2)
    def _():
        for copy in copies:
            copy.start()
        for copy in copies[:base]:
            copy.wait()

    @pl.when(section == 0)
    def _():
        tokens = TILE * HALF
        for k, v in enumerate(embed_rows(lat, inp, pos, (0, TILE - STRIDE), half)):
            acc[k * tokens : (k + 1) * tokens] = v
        norm[...] = normalise(acc[...], gain_ref[...])

    @pl.when(section < 2)
    def _():
        @pl.loop(0, chunks)
        def _(c):
            cut = pl.ds(pl.multiple_of(c * size, size), size)
            pltpu.make_async_copy(w1_h.at[0, :, cut], w1.at[:, cut], sems.at[base + 2 * c]).wait()
            pltpu.make_async_copy(w2_h.at[0, cut, :], w2.at[cut, :], sems.at[base + 2 * c + 1]).wait()

            @pl.when(section == 0)
            def _():
                h = gelu(jnp.dot(norm[...], w1[:, cut], preferred_element_type=F32)).astype(BF16)
                acc[...] += jnp.dot(h, w2[cut, :], preferred_element_type=F32)

    @pl.when(section == 0)
    def _():
        y[...] = acc[...].astype(BF16)

def table_kernel(anchors, out):
    a = anchors[...]
    column = lax.broadcasted_iota(jnp.int32, out.shape, 1) * STRIDE
    upper = lax.broadcasted_iota(jnp.int32, out.shape, 0) == 1
    table = jnp.where(upper, -1, 0)
    for k in range(a.shape[0]):
        row = jnp.broadcast_to(a[k : k + 1, 0:1], out.shape)
        here = jnp.broadcast_to(a[k : k + 1, 1:2], out.shape) == column
        table = jnp.where(here, jnp.where(upper, jnp.maximum(table, row), table + row), table)
    out[...] = table


def join_kernel(*refs):
    *tables, out = refs
    upper = lax.broadcasted_iota(jnp.int32, out.shape, 0) == 1
    total = tables[0][...]
    for table in tables[1:]:
        other = table[...]
        total = jnp.where(upper, jnp.maximum(total, other), total + other)
    out[...] = total


def tick_kernel(roles, outs, names, *refs):
    at = dict(zip(names, refs))
    section, slab = lax.axis_index("section"), lax.axis_index("win")
    parity = lax.rem(slab, 2)
    norm, acc = at["norm"], at["acc"]
    w1, w2 = at.get("new_w1", at["w1"]), at.get("new_w2", at["w2"])
    dim, hidden = w1.shape
    tokens = TILE * HALF

    def anchor_of(part):
        if part < 2:
            return part * STRIDE
        table = at["table"][...]
        slabs = table.shape[1]
        odd = lax.rem(slab + slabs - 1 + parity, slabs)
        here = lax.broadcasted_iota(jnp.int32, table.shape, 1) == odd
        upper = lax.broadcasted_iota(jnp.int32, table.shape, 0) == 1
        top = jnp.sum(jnp.where(here & upper, table, 0))
        return top if part == 2 else jnp.sum(jnp.where(here & ~upper, table, 0)) - top

    def rows_of(s):
        return pl.ds(0, tokens * len(roles[s]))

    def taken(name, s):
        size = tokens * len(roles[s])
        return at[name][pl.ds(tokens * (roles[s][0] % 2) % at[name].shape[0], size)]

    loads = [name for name in names if name.endswith("_h")]
    if loads:
        moves = []
        for k, name in enumerate(loads):
            whole, kept = at[name], at["new_" + name[:-2]]
            moves.append(
                pltpu.make_async_copy(whole.at[0] if whole.ndim > 2 else whole, kept, at["sems"].at[k])
            )

        @pl.when(section >= 2)
        def _():
            for move in moves[:3]:
                move.start()

            @pl.when(section == 3)
            def _():
                for move in moves[3:]:
                    move.start()

            for move in moves[:3]:
                move.wait()

        @pl.when(section == 3)
        def _():
            for move in moves[3:]:
                move.wait()

    if roles[0]:

        @pl.when(section == 0)
        def _():
            half = parity if roles[0][0] < 2 else 1 - parity
            where = [anchor_of(p) for p in roles[0]]
            for k, v in enumerate(embed_rows(at["lat"], at["inp"], at["pos"], where, half)):
                acc[k * tokens : (k + 1) * tokens] = v

    if roles[1]:

        @pl.when(section == 1)
        def _():
            acc[rows_of(1)] = taken("near1", 1).astype(F32)

    if roles[2]:

        @pl.when(section == 2)
        def _():
            acc[rows_of(2)] = taken("far2", 2).astype(F32)

    if roles[3]:

        @pl.when(section == 3)
        def _():
            acc[rows_of(3)] = jnp.dot(
                taken("near3", 3), at["skip"][:dim, :], preferred_element_type=F32
            ) + jnp.dot(taken("first3", 3), at["skip"][dim:, :], preferred_element_type=F32)

    for count in (1, 2):
        busy = [s for s in range(4) if len(roles[s]) == count]
        if not busy:
            continue
        assert busy == list(range(busy[0], busy[-1] + 1))

        @pl.when((section >= busy[0]) & (section <= busy[-1]))
        def _():
            rows = pl.ds(0, tokens * count)
            norm[rows] = normalise(acc[rows], at["gain"][...])
            size = hidden // 2

            def piece(c):
                cut = pl.ds(c * size, size)
                h = gelu(jnp.dot(norm[rows], w1[:, cut], preferred_element_type=F32)).astype(BF16)
                acc[rows] += jnp.dot(h, w2[cut, :], preferred_element_type=F32)

            if count == 1:
                piece(0)
                piece(1)
            else:
                pl.loop(0, 2)(piece)
            for name in sorted({outs[s] for s in busy if s < 3}):
                at[name][...] = acc[rows].astype(BF16)

    if roles[3]:
        totals = at["totals"]

        @pl.when(section == 3)
        def _():
            deep = acc[rows_of(3)].astype(BF16)
            noise = jnp.dot(deep, at["outp"][...], preferred_element_type=F32)
            noise = noise.astype(BF16).astype(F32)
            noise = noise.reshape(len(roles[3]), TILE, HALF, noise.shape[-1])
            if roles[3][0] == 0:
                totals[...] = jnp.zeros(totals.shape, F32)
            else:
                totals[...] = at["sums"][...]
            for k, part in enumerate(roles[3]):
                rows = pl.ds(anchor_of(part), TILE)
                totals[rows] = totals[rows] + noise[k]
            if roles[3][-1] == 3:
                row = lax.broadcasted_iota(jnp.int32, totals.shape, 0)
                count = jnp.zeros(totals.shape, F32)
                for k in range(4):
                    a = anchor_of(k)
                    count += ((row >= a) & (row < a + TILE)).astype(F32)
                band = totals.shape[0] // 4
                for k in range(4):
                    rows = slice(k * band, (k + 1) * band)
                    at[f"band{k}"][...] = (totals[rows] / count[rows]).astype(BF16)


def per_device(
    latent, anchors, in_proj, pos_embed, section_w1, section_w2, section_gain, skip_w, out_proj
):
    section = lax.axis_index("section")
    slab = lax.axis_index("win")
    sections, slabs = lax.axis_size("section"), lax.axis_size("win")
    height, width, feat = latent.shape
    dim = in_proj.shape[1]
    hidden = section_w1.shape[2]
    tokens = TILE * HALF
    axes = ("section", "win")
    positions = pos_embed.reshape(TILE, 2, HALF, dim)

    def hop(value, *pairs):
        return lax.ppermute(
            value, axes, [(a * slabs + w, b * slabs + w) for a, b in pairs for w in range(slabs)]
        )

    def swap(value):
        return hop(value, (0, 1), (1, 0), (2, 3), (3, 2))

    vmem = pl.BlockSpec(memory_space=pltpu.VMEM)
    hbm = pl.BlockSpec(memory_space=pltpu.HBM)
    any_space = pl.BlockSpec(memory_space=pl.ANY)

    def small_call(kernel, *given):
        return pl.pallas_call(
            kernel,
            out_shape=jax.ShapeDtypeStruct((2, slabs), jnp.int32),
            in_specs=[vmem] * len(given),
            out_specs=vmem,
            compiler_params=pltpu.CompilerParams(vmem_limit_bytes=MIB),
        )(*given)

    tables = [small_call(table_kernel, anchors)]
    def join(stride, extent):
        pairs = [
            [(w, w + stride * ((w // stride + k) % extent - w // stride % extent)) for w in range(slabs)]
            for k in range(1, extent)
        ]
        others = [lax.ppermute(tables[-1], "win", p) for p in pairs]
        tables.append(small_call(join_kernel, tables[-1], *others))

    join(*ROUNDS[0])

    chunks = 5
    flops = 4 * tokens * dim * hidden

    def act(parts):
        return pltpu.VMEM((parts * tokens, dim), BF16)

    def room(parts):
        return [pltpu.VMEM((parts * tokens, dim), BF16), pltpu.VMEM((parts * tokens, dim), F32)]

    def like(a, shape=None):
        return jax.ShapeDtypeStruct(shape or a.shape, a.dtype)

    def held(a, shape=None):
        return pltpu.VMEM(shape or a.shape, a.dtype)

    def pinned(a):
        return pltpu.with_memory_space_constraint(a, pltpu.VMEM)

    y0, lat, inp, pos, gain, w1, w2 = pl.pallas_call(
        functools.partial(load_kernel, chunks),
        out_shape=[
            act(2), held(latent), held(in_proj), held(positions), held(section_gain),
            held(section_w1, (dim, hidden)), held(section_w2, (hidden, dim)),
        ],
        in_specs=[hbm] * 6,
        out_specs=[vmem] * 7,
        scratch_shapes=room(2) + [pltpu.SemaphoreType.DMA((4 + 2 * chunks,))],
        compiler_params=pltpu.CompilerParams(vmem_limit_bytes=16 * MIB),
    )(
        *(
            pltpu.with_memory_space_constraint(a, pltpu.HBM)
            for a in (
                latent, in_proj, positions, section_gain, section_w1, section_w2
            )
        ),
    )

    lat, inp, pos, gain, w1, w2 = map(pinned, (lat, inp, pos, gain, w1, w2))
    held_now = dict(gain=gain, w1=w1, w2=w2)
    last_loads = dict(
        gain_h=section_gain, w1_h=section_w1, w2_h=section_w2, skip_h=skip_w, outp_h=out_proj
    )
    late = {}

    def tick(roles, outs, after=(), load={}, **extra):
        roles = [roles.get(s, ()) for s in range(4)]
        outs = [outs.get(s) for s in range(4)]
        given = {**held_now, **({k: late[k] for k in held_now} if late else {})}
        if any(p >= 2 for p in (*roles[0], *roles[3])):
            given["table"] = tables[-1]
        if roles[0]:
            given.update(lat=lat, inp=inp, pos=pos)
        if roles[3]:
            given.update(late)
        given.update({k: pinned(a) for k, a in extra.items()})
        specs = [vmem] * len(given) + [any_space] * len(after)
        if load:
            given.update(
                {k: pltpu.with_memory_space_constraint(a, pltpu.HBM) for k, a in load.items()}
            )
            specs += [hbm] * len(load)
        given.update({f"after{k}": a for k, a in enumerate(after)})
        made = {outs[s]: act(len(roles[s])) for s in range(3) if roles[s]}
        aliases = {}
        scratch = dict(zip(("norm", "acc"), room(max(map(len, roles)))))
        if load:
            made.update({"new_" + k[:-2]: held(a, a.shape[-2:]) for k, a in load.items()})
            aliases = {
                list(given).index(k): list(made).index("new_" + k) for k in held_now
            }
            scratch["sems"] = pltpu.SemaphoreType.DMA((len(load),))
        if roles[3] and roles[3][-1] == 3:
            for k in range(sections):
                made[f"band{k}"] = like(latent, (height // sections, *latent.shape[1:]))
            scratch["totals"] = pltpu.VMEM(latent.shape, F32)
        elif roles[3]:
            made["totals"] = pltpu.VMEM(latent.shape, F32)
        results = pl.pallas_call(
            functools.partial(tick_kernel, roles, outs, [*given, *made, *scratch]),
            out_shape=list(made.values()),
            in_specs=specs,
            out_specs=[vmem] * len(made),
            scratch_shapes=list(scratch.values()),
            input_output_aliases=aliases,
            cost_estimate=pl.CostEstimate(
                flops=COST * sum(map(len, roles)) * flops,
                bytes_accessed=MIB,
                transcendentals=0,
            ),
            compiler_params=pltpu.CompilerParams(vmem_limit_bytes=16 * MIB),
        )(*given.values())
        return dict(zip(made, results))

    y0, _ = lax.optimization_barrier((y0, tables[1]))
    near01 = swap(y0)
    first01 = hop(y0, (0, 3))
    k1 = tick({1: (0, 1)}, {1: "y"}, near1=near01, load=last_loads)
    late.update({name[:-2]: pinned(k1["new_" + name[:-2]]) for name in last_loads})
    far01 = hop(k1["y"], (1, 2))
    tables[1], _ = lax.optimization_barrier((tables[1], k1["y"]))
    for stride, extent in ROUNDS[1:]:
        join(stride, extent)
    f2 = tick({0: (2,)}, {0: "y"}, after=[first01, far01])["y"]
    near2 = hop(f2, (0, 1))
    first2 = hop(f2, (0, 3))
    s2 = tick({1: (2,)}, {1: "y"}, near1=near2)["y"]
    far2 = hop(s2, (1, 2))
    f3 = tick({0: (3,)}, {0: "y"}, after=[s2])["y"]
    near3 = swap(f3)
    first3 = hop(f3, (0, 3))
    t01 = tick({2: (0, 1)}, {2: "t"}, far2=far01, after=[f3])["t"]
    third01 = swap(t01)
    s3 = tick({1: (3,)}, {1: "y"}, near1=near3, after=[t01])["y"]
    far3 = hop(s3, (1, 2))
    d01 = tick({3: (0, 1)}, {}, near3=third01, first3=first01, after=[s3])["totals"]
    t2 = tick({2: (2,)}, {2: "t"}, far2=far2, after=[d01])["t"]
    third2 = swap(t2)
    t3 = tick({2: (3,)}, {2: "t"}, far2=far3, after=[t2])["t"]
    d2 = tick({3: (2,)}, {}, near3=third2, first3=first2, sums=d01)["totals"]
    t3, _ = lax.optimization_barrier((t3, d2))
    third3 = swap(t3)
    bands = tick({3: (3,)}, {}, near3=third3, first3=first3, sums=d2)
    sent = {s: hop(bands[f"band{s}"], (3, s)) for s in (0, 1, 2)}
    result = bands["band3"]
    for s in (2, 1, 0):
        result = jnp.where(section == s, sent[s], result)
    return result


def solution(mesh):
    placed = (
        P(None, "win", None),
        P("win", None),
        P(),
        P(),
        P("section", None, None),
        P("section", None, None),
        P("section", None),
        P(),
        P(),
    )
    return jax.shard_map(
        per_device, mesh=mesh, in_specs=placed, out_specs=P("section", "win", None), check_vma=False
    )
```
